128 devices in a mesh: fsdp: 16 (over x, y_hi, core), node: 8 (over y_lo, z).
Axes of the slice: x: 4, y: 4 (y_hi: 2, y_lo: 2; y = y_hi * 2 + y_lo), z: 4, core: 2. Of those that a mesh axis runs over, the one named last changes fastest.
Arguments:
- activations: bfloat16 [8192, 8192], P('fsdp', 'node'), may hold values from -6 to 6
- qkv_weight: bfloat16 [8192, 5120], P('fsdp', 'node'), may hold values from -0.09375 to 0.09375
- qkv_grad: bfloat16 [8192, 5120], P('fsdp', 'node'), may hold values from -6 to 6
Outputs:
- projected: bfloat16 [8192, 5120], P('fsdp', 'node')
- input_grad: bfloat16 [8192, 8192], P('fsdp', 'node')
- weight_grad: float32 [8192, 5120], P('fsdp', 'node')
The draws below stay inside these ranges and needn't reach their ends.
All inputs are finite; a program needn't handle non-finite values.
Results may differ from the reference program's by a relative error of at most 0.017.
Values may be sent and summed in bfloat16 or wider, within the bound.
No kernel may reach another device: no remote copies, remote signals or barrier semaphores. Data moves between devices by JAX's collectives and lax.ppermute only.
A program may use at most 128 MiB of HBM per device.

```python
import jax
import jax.numpy as jnp
from jax import lax

D = 8192
TOK = 512
C = 5120
TOKENS = 8192
N_FSDP = 16
N_NODE = 8


def raised(values, own_key, source, target, parts, factor):
    def block_of(axis_at):
        return (jnp.arange(values.shape[axis_at]) // (values.shape[axis_at] // parts)).reshape((-1,) + (1,) * (values.ndim - 1 - axis_at))

    first = jax.random.permutation(own_key, parts)[block_of(target)]
    far = (block_of(target) + parts // 2) % parts
    return jnp.where((block_of(source) == first) | (block_of(source) == far), factor * values, values)


def level_of(rng, dims, shards, smallest, top_value):
    def one(position, shards_of):
        heights = jax.random.uniform(jax.random.fold_in(jax.random.fold_in(rng, 6), position), (shards_of,), jnp.float32, smallest / len(shards), top_value / len(shards))
        return jnp.repeat(jnp.exp(heights), dims[position] // shards_of).reshape((-1,) + (1,) * (len(dims) - position - 1))

    factor_of = one(*shards[0])
    for cut in shards[1:]:
        factor_of = factor_of * one(*cut)
    return factor_of


def centred(key, extent, scale, reach, pieces=(), held_as=jnp.bfloat16):
    array = jax.random.normal(key, extent, jnp.float32) * scale
    if len(pieces) > 0:
        array = level_of(key, extent, pieces, -0.22, 0.18) * array
    return jnp.clip(array, min=-reach, max=reach).astype(held_as)


def bell_draw_with(rng, extent, scale, reach, cuts, heavy, kind=jnp.bfloat16):
    array = scale * jax.random.normal(rng, extent, jnp.float32)
    if cuts:
        array = array * level_of(rng, extent, cuts, -0.22, 0.18)
    return jnp.clip(raised(array, jax.random.fold_in(rng, 3), *heavy), -reach, reach).astype(kind)


def setup_inputs(seed: int = 0) -> dict:
    splits = jax.random.split(jax.random.key(seed), 4)
    return {
        "activations": bell_draw_with(splits[0], (TOKENS, D), 1.0, 6.0, ((0, 16), (1, 8)), (0, 1, 16, 2.0)),
        "qkv_weight": bell_draw_with(splits[1], (D, C), D ** -0.5, 0.09375, ((0, 16), (1, 8)), (1, 0, 16, 2.0)),
        "qkv_grad": centred(splits[2], (TOKENS, C), 1.0, 6.0, ((0, 16), (1, 8))),
    }


def reference(activations, qkv_weight, qkv_grad):
    projected = jnp.dot(activations, qkv_weight, preferred_element_type=jnp.float32).astype(jnp.bfloat16)
    block = C // N_NODE
    total = jnp.zeros((TOKENS, D), jnp.float32)
    for index in range(N_NODE):
        grad_block = qkv_grad[:, index * block:(index + 1) * block]
        weight_block = qkv_weight[:, index * block:(index + 1) * block]
        partial_block = lax.dot_general(grad_block, weight_block, (((1,), (1,)), ((), ())), preferred_element_type=jnp.float32)
        total = total + partial_block.astype(jnp.bfloat16).astype(jnp.float32)
    input_grad = total.astype(jnp.bfloat16)

    def add_group(index, carry):
        rows_in = lax.dynamic_slice_in_dim(activations, index * TOK, TOK, 0)
        grads_in = lax.dynamic_slice_in_dim(qkv_grad, index * TOK, TOK, 0)
        term = lax.dot_general(rows_in, grads_in, (((0,), (0,)), ((), ())), preferred_element_type=jnp.float32)
        return carry + term.astype(jnp.bfloat16).astype(jnp.float32)

    weight_grad = lax.fori_loop(0, N_FSDP, add_group, jnp.zeros((D, C), jnp.float32))
    return projected, input_grad, weight_grad
```

```python
import functools

import jax
import jax.numpy as jnp
from jax import lax
from jax.experimental import pallas as pl
from jax.experimental.pallas import tpu as pltpu
from jax.sharding import PartitionSpec as P

AXES = ("fsdp", "node")
BF16, F32 = jnp.bfloat16, jnp.float32


def flip(value, x=0, y=0, z=0, c=0):
    pairs = []
    for i in range(128):
        p, q = divmod(i, 8)
        px, py, pc = p // 4, (p // 2 % 2) * 2 + q // 4, p % 2
        px, py, pz, pc = px ^ x, py ^ y, q % 4 ^ z, pc ^ c
        pairs.append((i, ((px * 2 + py // 2) * 2 + pc) * 8 + py % 2 * 4 + pz))
    return lax.ppermute(value, AXES, pairs)


def add(*terms):
    total = terms[0].astype(F32)
    for term in terms[1:]:
        total = total + term.astype(F32)
    return total


def gather4(value, axis):
    one, three = flip(value, **{axis: 1}), flip(value, **{axis: 3})
    half = value.shape[0] // 2
    far = [flip(three[:half], **{axis: 1}), flip(one[half:], **{axis: 3})]
    return [value, one, jnp.concatenate(far, 0), three]


def scatter4(pieces, axis):
    (own_t, own_b), (one_t, one_b), (far_t, far_b), (three_t, three_b) = pieces
    top3 = flip(far_t, **{axis: 1})
    bottom1 = flip(far_b, **{axis: 3})
    got1_t = flip(one_t, **{axis: 1})
    got3_b = flip(three_b, **{axis: 3})
    got1_b = flip(add(one_b, bottom1).astype(BF16), **{axis: 1})
    got3_t = flip(add(three_t, top3).astype(BF16), **{axis: 3})
    return add(own_t, got1_t, got3_t), add(own_b, got1_b, got3_b)


def dw_kernel(m, a, g, out):
    out[0] = lax.dot_general(a[0], g[...], (((0,), (0,)), ((), ())), preferred_element_type=F32).astype(BF16)


def weight_terms(mask, a, g):
    n, t, d = a.shape
    return pl.pallas_call(
        dw_kernel,
        grid_spec=pltpu.PrefetchScalarGridSpec(
            num_scalar_prefetch=1,
            grid=(n,),
            in_specs=[
                pl.BlockSpec((1, t, d), lambda k, m: (k ^ m[0], 0, 0)),
                pl.BlockSpec(g.shape, lambda k, m: (0, 0)),
            ],
            out_specs=pl.BlockSpec((1, d, g.shape[1]), lambda k, m: (k, 0, 0)),
        ),
        out_shape=jax.ShapeDtypeStruct((n, d, g.shape[1]), BF16),
        compiler_params=pltpu.CompilerParams(vmem_limit_bytes=32 << 20),
        name="weight_terms",
    )(mask, a, g)


def da_kernel(m, g, w1, w2, out):
    i = pl.program_id(0) ^ m[0]
    n = w1.shape[2]
    contract = (((1,), (1,)), ((), ()))

    @pl.when(i % 2 == 0)
    def _():
        total = lax.dot_general(g[:, :n], w1[0], contract, preferred_element_type=F32)
        total += lax.dot_general(g[:, n:], w2[0, 0], contract, preferred_element_type=F32)
        out[0] = total.astype(BF16)

    @pl.when(i % 2 == 1)
    def _():
        total = lax.dot_general(g[:, :n], w2[0, 1], contract, preferred_element_type=F32)
        total += lax.dot_general(g[:, n:], w2[0, 2], contract, preferred_element_type=F32)
        out[0] = total.astype(BF16)


def input_terms(mask, g, w1, w2):
    t, d = g.shape[0], w1.shape[1]
    return pl.pallas_call(
        da_kernel,
        grid_spec=pltpu.PrefetchScalarGridSpec(
            num_scalar_prefetch=1,
            grid=(8,),
            in_specs=[
                pl.BlockSpec(g.shape, lambda i, m: (0, 0)),
                pl.BlockSpec((1, *w1.shape[1:]), lambda i, m: ((i ^ m[0]) // 2, 0, 0)),
                pl.BlockSpec((1, *w2.shape[1:]), lambda i, m: ((i ^ m[0]) // 2, 0, 0, 0)),
            ],
            out_specs=pl.BlockSpec((1, t, d), lambda i, m: (i, 0, 0)),
        ),
        out_shape=jax.ShapeDtypeStruct((8, t, d), BF16),
        compiler_params=pltpu.CompilerParams(vmem_limit_bytes=32 << 20),
        name="input_terms",
    )(mask, g, w1, w2)


def fwd_kernel(m, a0, a1, w1, w2, out, total):
    k = pl.program_id(0)
    n = w1.shape[2]

    def dot(left, right):
        return jnp.dot(left, right, preferred_element_type=F32)

    own = dot(a0[0], w1[0]) + dot(a1[0], w2[0, 1])
    other = dot(a0[0], w2[0, 0]) + dot(a1[0], w2[0, 2])

    @pl.when(k == 0)
    def _():
        total[:, :n] = own
        total[:, n:] = other

    @pl.when(k > 0)
    def _():
        total[:, :n] += own
        total[:, n:] += other

    @pl.when(k == 3)
    def _():
        out[...] = total[...].astype(BF16)


def forward_terms(mask, a, w1, w2):
    t, d, n = a.shape[1], a.shape[2], w1.shape[2]
    return pl.pallas_call(
        fwd_kernel,
        grid_spec=pltpu.PrefetchScalarGridSpec(
            num_scalar_prefetch=1,
            grid=(4,),
            in_specs=[
                pl.BlockSpec((1, t, d), lambda k, m: ((2 * k) ^ m[0], 0, 0)),
                pl.BlockSpec((1, t, d), lambda k, m: ((2 * k + 1) ^ m[0], 0, 0)),
                pl.BlockSpec((1, *w1.shape[1:]), lambda k, m: (k, 0, 0)),
                pl.BlockSpec((1, *w2.shape[1:]), lambda k, m: (k, 0, 0, 0)),
            ],
            out_specs=pl.BlockSpec((t, 2 * n), lambda k, m: (0, 0)),
            scratch_shapes=[pltpu.VMEM((t, 2 * n), F32)],
        ),
        out_shape=jax.ShapeDtypeStruct((t, 2 * n), BF16),
        compiler_params=pltpu.CompilerParams(vmem_limit_bytes=40 << 20),
        name="forward_terms",
    )(mask, a, a, w1, w2)


def body(activations, qkv_weight, qkv_grad):
    p, q = lax.axis_index("fsdp"), lax.axis_index("node")
    x, y_hi, c, y_lo, z = p // 4, p // 2 % 2, p % 2, q // 4, q % 4
    mask = ((x // 2 ^ y_lo) * 4 + (x % 2 ^ z // 2) * 2 + (y_hi ^ z % 2)).astype(jnp.int32).reshape(1)
    tok, wide = activations.shape
    cols = qkv_grad.shape[1]
    sub = wide // 4

    w_keep = lax.dynamic_slice_in_dim(qkv_weight, c * sub, sub, 0)
    w_got = flip(lax.dynamic_slice_in_dim(qkv_weight, (1 - c) * sub, sub, 0), c=1)
    same = c == y_lo
    w_same, w_diff = jnp.where(same, w_keep, w_got), jnp.where(same, w_got, w_keep)
    w_y1, w_y3, w_y2 = flip(w_diff, y=1), flip(w_diff, y=3), flip(w_same, y=2)

    a_keep = lax.dynamic_slice_in_dim(activations, y_lo * 2 * sub, 2 * sub, 1)
    a_y = flip(lax.dynamic_slice_in_dim(activations, (1 - y_lo) * 2 * sub, 2 * sub, 1), y=1)
    g_y = flip(qkv_grad, y=1)

    def by_core(a):
        mine = lax.dynamic_slice_in_dim(a, c * sub, sub, 1)
        theirs = flip(lax.dynamic_slice_in_dim(a, (1 - c) * sub, sub, 1), c=1)
        return jnp.concatenate([mine, theirs], 0)

    a0 = gather4(by_core(a_keep), "z")
    w1 = jnp.stack(gather4(w_same, "x"))
    a1 = gather4(by_core(a_y), "z")
    a = jnp.stack(a0 + a1)
    w2 = jnp.stack(gather4(jnp.concatenate([w_y1, w_y2, w_y3], 0), "x")).reshape(4, 3, sub, cols)
    g_rows = jnp.concatenate([qkv_grad, g_y], 1)
    g = jnp.concatenate([g_rows, flip(g_rows, c=1)], 0)

    dw = weight_terms(mask, a, g)
    dw_top, dw_bottom = scatter4([(dw[2 * k], dw[2 * k + 1]) for k in range(4)], "x")
    dw_00 = dw_top[:, :cols]
    dw_y1 = flip(dw_top[:, cols:].astype(BF16), y=1)
    dw_y2 = flip(dw_bottom[:, :cols].astype(BF16), y=2)
    dw_y3 = flip(dw_bottom[:, cols:].astype(BF16), y=3)
    b_same, b_diff = add(dw_00, dw_y2), add(dw_y1, dw_y3)
    b_keep = jnp.where(same, b_same, b_diff)
    b_got = flip(jnp.where(same, b_diff, b_same).astype(BF16), c=1).astype(F32)
    weight_grad = jnp.where(c == 0, jnp.concatenate([b_keep, b_got], 0), jnp.concatenate([b_got, b_keep], 0))

    da = input_terms(mask, g, w1, w2)
    da_keep, da_send = scatter4([(da[k], da[4 + k]) for k in range(4)], "z")
    da_y = flip(da_send.astype(BF16), y=1)
    da_keep = da_keep.astype(BF16)
    da_h0, da_h1 = jnp.where(y_lo == 0, da_keep, da_y), jnp.where(y_lo == 0, da_y, da_keep)
    both = jnp.concatenate([da_h0, da_h1], 1)
    mine, theirs = both[:tok], flip(both[tok:], c=1)
    r0, r1 = jnp.where(c == 0, mine, theirs), jnp.where(c == 0, theirs, mine)
    input_grad = jnp.concatenate([r0[:, :sub], r1[:, :sub], r0[:, sub:], r1[:, sub:]], 1)

    fwd = forward_terms(mask, a, w1, w2)
    fwd = add(fwd[:tok], flip(fwd[tok:], c=1))
    projected = add(fwd[:, :cols], flip(fwd[:, cols:].astype(BF16), y=1)).astype(BF16)
    return projected, input_grad, weight_grad


def solution(mesh):
    spec = P("fsdp", "node")
    return jax.shard_map(body, mesh=mesh, in_specs=(spec,) * 3, out_specs=(spec,) * 3, check_vma=False)
```

```python
import functools

import jax
import jax.numpy as jnp
from jax import lax
from jax.experimental import pallas as pl
from jax.experimental.pallas import tpu as pltpu
from jax.sharding import PartitionSpec as P

AXES = ("fsdp", "node")
BF16, F32 = jnp.bfloat16, jnp.float32
FAR = 2


def flip(value, x=0, y=0, z=0, c=0):
    pairs = []
    for i in range(128):
        p, q = divmod(i, 8)
        place = p // 4, (p // 2 % 2) * 2 + q // 4, q % 4, p % 2
        bits = [b if isinstance(b, int) else b[place[3]] for b in (x, y, z, c)]
        px, py, pz, pc = (a ^ b for a, b in zip(place, bits, strict=True))
        pairs.append((i, ((px * 2 + py // 2) * 2 + pc) * 8 + py % 2 * 4 + pz))
    return lax.ppermute(value, AXES, pairs)


ONE, TWO = (1, 3), (3, 1)


def tie(*values):
    return lax.optimization_barrier(values)


def add(*terms):
    total = terms[0].astype(F32)
    for term in terms[1:]:
        total = total + term.astype(F32)
    return total


def gather4(value, axis):
    one, two = flip(value, **{axis: ONE}), flip(value, **{axis: TWO})
    half = value.shape[0] // 2
    far = [flip(two[:half], **{axis: ONE}), flip(one[half:], **{axis: TWO})]
    return [value, one, jnp.concatenate(far, 0), two]


def scatter4(far_one, far_two, one, two, own, axis):
    got_one, got_two = flip(far_one, **{axis: ONE}), flip(far_two, **{axis: TWO})
    got_bottom1 = flip(add(one[0], got_two[0]).astype(BF16), **{axis: ONE})
    got_top2 = flip(add(two[0], got_one[0]).astype(BF16), **{axis: TWO})
    return add(own[0], got_one[1], got_top2), add(own[1], got_two[1], got_bottom1)


def pieces_of(top, bottom):
    return [[top(2), top(1)], [bottom(2), bottom(3)], [bottom(1)], [top(3)], [top(0), bottom(0)]]


def pick(k, values):
    chosen = values[0]
    for at in range(1, len(values)):
        chosen = jnp.where(k == at, values[at], chosen)
    return chosen


def cost(products):
    return pl.CostEstimate(flops=4 * products, bytes_accessed=products // 512, transcendentals=0)


def turned(slot, m):
    return slot ^ ((slot & 1) * m[1])


def a_block(xs, yh, m):
    i = (turned(xs, m) * 2 + yh) ^ m[0]
    return i // 4 * 4 + turned(i % 4, m)


def w_block(ylo, zs, m):
    i = (ylo * 4 + turned(zs, m)) ^ m[0]
    return turned(i // 2, m), i % 2


def sub_of(yh, ylo, m):
    return turned(yh * 2 + ylo, m)


def put(step, groups, outs, store):
    at = 0
    for group, out in zip(groups, outs, strict=True):
        for place in range(len(group)):

            @pl.when(step == at)
            def _():
                store(out.at[place])

            at += 1


def dw_kernel(groups, m, a, g, *outs):
    block = lax.dot_general(a[0], g[...], (((0,), (0,)), ((), ())), preferred_element_type=F32).astype(BF16)
    cols = block.shape[1] // 2

    def store(out):
        out[0] = block[:, :cols]
        out[1] = block[:, cols:]

    put(pl.program_id(0), groups, outs, store)


def weight_terms(scalars, a, g):
    _, t, d = a.shape
    cols = g.shape[1] // 2
    groups = pieces_of(lambda slot: (slot, 0), lambda slot: (slot, 1))
    blocks = sum(groups, [])

    def a_index(k, m):
        return (a_block(pick(k, [b[0] for b in blocks]), pick(k, [b[1] for b in blocks]), m), 0, 0)

    return pl.pallas_call(
        functools.partial(dw_kernel, groups),
        grid_spec=pltpu.PrefetchScalarGridSpec(
            num_scalar_prefetch=1,
            grid=(8,),
            in_specs=[pl.BlockSpec((1, t, d), a_index), pl.BlockSpec(g.shape, lambda k, m: (0, 0))],
            out_specs=[pl.BlockSpec((len(group), 2, d, cols), lambda k, m: (0, 0, 0, 0)) for group in groups],
        ),
        out_shape=[jax.ShapeDtypeStruct((len(group), 2, d, cols), BF16) for group in groups],
        compiler_params=pltpu.CompilerParams(vmem_limit_bytes=32 << 20),
        cost_estimate=cost(8 * t * d * 2 * cols),
        name="weight_terms",
    )(scalars, a, g)


def da_kernel(groups, m, g, w0, w1, *outs):
    cols = w0.shape[-1]
    contract = (((1,), (1,)), ((), ()))
    block = lax.dot_general(g[:, :cols], w0[0, 0], contract, preferred_element_type=F32)
    block += lax.dot_general(g[:, cols:], w1[0, 0], contract, preferred_element_type=F32)
    block = block.astype(BF16)

    def store(out):
        out[...] = block

    put(pl.program_id(0), groups, outs, store)


def input_terms(scalars, g, w):
    t, d, cols = g.shape[0], w.shape[2], w.shape[3]
    groups = pieces_of(lambda slot: (0, slot), lambda slot: (1, slot))
    blocks = sum(groups, [])

    def w_index(ylo, k, m):
        xs, yh = w_block(pick(k, [b[0] for b in blocks]), pick(k, [b[1] for b in blocks]), m)
        return (xs, sub_of(yh, ylo, m), 0, 0)

    return pl.pallas_call(
        functools.partial(da_kernel, groups),
        grid_spec=pltpu.PrefetchScalarGridSpec(
            num_scalar_prefetch=1,
            grid=(8,),
            in_specs=[
                pl.BlockSpec(g.shape, lambda k, m: (0, 0)),
                pl.BlockSpec((1, 1, d, cols), functools.partial(w_index, 0)),
                pl.BlockSpec((1, 1, d, cols), functools.partial(w_index, 1)),
            ],
            out_specs=[pl.BlockSpec((len(group), t, d), lambda k, m: (0, 0, 0)) for group in groups],
        ),
        out_shape=[jax.ShapeDtypeStruct((len(group), t, d), BF16) for group in groups],
        compiler_params=pltpu.CompilerParams(vmem_limit_bytes=32 << 20),
        cost_estimate=cost(8 * t * d * 2 * cols),
        name="input_terms",
    )(scalars, g, w, w)


def fwd_kernel(m, a0, a1, w, mine, theirs, total):
    k = pl.program_id(0)
    cols = w.shape[-1]
    t = mine.shape[0]

    def dot(left, right):
        return jnp.dot(left, right, preferred_element_type=F32)

    for ylo in range(2):
        s0, s1 = sub_of(0, ylo, m), sub_of(1, ylo, m)
        part = dot(a0[0], w[0, s0]) + dot(a1[0], w[0, s1])
        at = slice(ylo * cols, (ylo + 1) * cols)

        @pl.when(k == 0)
        def _():
            total[:, at] = part

        @pl.when((k > 0) & (k < 3))
        def _():
            total[:, at] += part

        @pl.when(k == 3)
        def _():
            final = (total[:, at] + part).astype(BF16)
            mine[:, at] = final[:t]
            theirs[:, at] = final[t:]


def forward_terms(scalars, a, w):
    t, d, cols = a.shape[1], a.shape[2], w.shape[3]
    return pl.pallas_call(
        fwd_kernel,
        grid_spec=pltpu.PrefetchScalarGridSpec(
            num_scalar_prefetch=1,
            grid=(4,),
            in_specs=[
                pl.BlockSpec((1, t, d), lambda k, m: (a_block(k, 0, m), 0, 0)),
                pl.BlockSpec((1, t, d), lambda k, m: (a_block(k, 1, m), 0, 0)),
                pl.BlockSpec((1, *w.shape[1:]), lambda k, m: (k, 0, 0, 0)),
            ],
            out_specs=[pl.BlockSpec((t // 2, 2 * cols), lambda k, m: (0, 0))] * 2,
            scratch_shapes=[pltpu.VMEM((t, 2 * cols), F32)],
        ),
        out_shape=[jax.ShapeDtypeStruct((t // 2, 2 * cols), BF16)] * 2,
        compiler_params=pltpu.CompilerParams(vmem_limit_bytes=40 << 20),
        cost_estimate=cost(8 * t * d * 2 * cols),
        name="forward_terms",
    )(scalars, a, a, w)


def body(activations, qkv_weight, qkv_grad):
    p, q = lax.axis_index("fsdp"), lax.axis_index("node")
    x, y_hi, c, y_lo, z = p // 4, p // 2 % 2, p % 2, q // 4, q % 4
    mask = (x // 2 ^ y_lo) * 4 + (x % 2 ^ z // 2) * 2 + (y_hi ^ z % 2)
    scalars = jnp.stack([mask, 2 * c]).astype(jnp.int32)
    tok, wide = activations.shape
    cols = qkv_grad.shape[1]
    sub = wide // 4

    w_same = lax.dynamic_slice_in_dim(qkv_weight, y_lo * sub, sub, 0)
    w_diff = lax.dynamic_slice_in_dim(qkv_weight, (1 - y_lo) * sub, sub, 0)
    ws_one, ws_two = flip(w_same, x=ONE), flip(w_same, x=TWO)
    w_one, w_two = flip(w_diff, y=ONE), flip(w_diff, y=TWO)
    ws_one, ws_two, w_same = tie(ws_one, ws_two, w_same)
    w_far = flip(w_same, y=2)

    halves = [activations[:, : 2 * sub], activations[:, 2 * sub :]]
    a_mine, a_theirs = jnp.where(c == 0, halves[0], halves[1]), jnp.where(c == 0, halves[1], halves[0])
    a_rows = jnp.concatenate([a_mine, flip(a_theirs, c=1)], 0)
    a_keep = lax.dynamic_slice_in_dim(a_rows, y_lo * sub, sub, 1)
    a_send = lax.dynamic_slice_in_dim(a_rows, (1 - y_lo) * sub, sub, 1)
    w_one, a_send = tie(w_one, a_send)
    a_y = flip(a_send, y=1)
    w_near = jnp.concatenate([w_one, w_far, w_two], 0)
    wn_one, wn_two = flip(w_near, x=ONE), flip(w_near, x=TWO)
    ka_one, ka_two = flip(a_keep, z=ONE), flip(a_keep, z=TWO)
    a_y, grad = tie(a_y, qkv_grad)
    g_y = flip(grad, y=1)
    ya_one, ya_two = flip(a_y, z=ONE), flip(a_y, z=TWO)
    far_one, far_two = flip(ka_two[:tok], z=ONE), flip(ka_one[tok:], z=TWO)
    ka_far = jnp.concatenate([far_one, far_two], 0)
    far_one, far_two = flip(ya_two[:tok], z=ONE), flip(ya_one[tok:], z=TWO)
    ya_far = jnp.concatenate([far_one, far_two], 0)
    a = jnp.stack([a_keep, ka_one, ka_far, ka_two, a_y, ya_one, ya_far, ya_two])

    w_own, w_1, w_2 = (jnp.concatenate(v, 0) for v in ((w_same, w_near), (ws_one, wn_one), (ws_two, wn_two)))
    w_2far = jnp.concatenate([flip(w_2[: 2 * sub], x=ONE), flip(w_1[2 * sub :], x=TWO)], 0)
    w = jnp.stack([w_own, w_1, w_2far, w_2]).reshape(4, 4, sub, cols)
    g_rows = jnp.concatenate([grad, g_y], 1)
    g = jnp.concatenate([g_rows, flip(g_rows, c=1)], 0)

    dw_first, *dw = weight_terms(scalars, a, g)
    dw_first, scalars = tie(dw_first, scalars)
    da_first, *da = input_terms(scalars, g, w)
    da_first, scalars = tie(da_first, scalars)
    da_keep, da_send = scatter4(da_first, *da, "z")
    dw_0, dw_1 = scatter4(dw_first, *dw, "x")

    mine, theirs = forward_terms(scalars, a, w)
    fwd = add(mine, flip(theirs, c=1))
    fwd_y = flip(fwd[:, cols:].astype(BF16), y=1)
    fwd_y, da_send = tie(fwd_y, da_send)
    projected = add(fwd[:, :cols], fwd_y).astype(BF16)

    da_y = flip(da_send.astype(BF16), y=1)
    da_keep = da_keep.astype(BF16)
    r0, r1 = jnp.where(y_lo == 0, da_keep, da_y), jnp.where(y_lo == 0, da_y, da_keep)
    both = jnp.concatenate([r0, r1], 1)
    mine, theirs = both[:tok], flip(both[tok:], c=1)
    input_grad = jnp.concatenate([jnp.where(c == 0, mine, theirs), jnp.where(c == 0, theirs, mine)], 1)

    send1, send3 = dw_0[1].astype(BF16), dw_1[1].astype(BF16)
    got_one = flip(jnp.where(c == 0, send1, send3), y=ONE)
    got_two = flip(jnp.where(c == 0, send3, send1), y=TWO)
    got_far = flip(dw_1[0].astype(BF16), y=2)
    same, diff = add(dw_0[0], got_far), add(got_one, got_two)
    weight_grad = jnp.where(y_lo == 0, jnp.concatenate([same, diff], 0), jnp.concatenate([diff, same], 0))

    return projected, input_grad, weight_grad


def solution(mesh):
    spec = P("fsdp", "node")
    return jax.shard_map(body, mesh=mesh, in_specs=(spec,) * 3, out_specs=(spec,) * 3, check_vma=False)
```

```python
import functools

import jax
import jax.numpy as jnp
from jax import lax
from jax.experimental import pallas as pl
from jax.experimental.pallas import tpu as pltpu
from jax.sharding import PartitionSpec as P

AXES = ("fsdp", "node")
BF16, F32 = jnp.bfloat16, jnp.float32
FAR = 2


def flip(value, x=0, y=0, z=0, c=0):
    pairs = []
    for i in range(128):
        p, q = divmod(i, 8)
        place = p // 4, (p // 2 % 2) * 2 + q // 4, q % 4, p % 2
        bits = [b if isinstance(b, int) else b[place[3]] for b in (x, y, z, c)]
        px, py, pz, pc = (a ^ b for a, b in zip(place, bits, strict=True))
        pairs.append((i, ((px * 2 + py // 2) * 2 + pc) * 8 + py % 2 * 4 + pz))
    return lax.ppermute(value, AXES, pairs)


ONE, TWO = (1, 3), (3, 1)


def tie(*values):
    return lax.optimization_barrier(values)


def add(*terms):
    total = terms[0].astype(F32)
    for term in terms[1:]:
        total = total + term.astype(F32)
    return total


def gather4(value, axis):
    one, two = flip(value, **{axis: ONE}), flip(value, **{axis: TWO})
    half = value.shape[0] // 2
    far = [flip(two[:half], **{axis: ONE}), flip(one[half:], **{axis: TWO})]
    return [value, one, jnp.concatenate(far, 0), two]


def scatter4(far_one, far_two, one, two, own, axis):
    got_one, got_two = flip(far_one, **{axis: ONE}), flip(far_two, **{axis: TWO})
    got_bottom1 = flip(add(one[0], got_two[0]).astype(BF16), **{axis: ONE})
    got_top2 = flip(add(two[0], got_one[0]).astype(BF16), **{axis: TWO})
    return add(own[0], got_one[1], got_top2), add(own[1], got_two[1], got_bottom1)


def pieces_of(top, bottom):
    return [[top(2), top(1)], [bottom(2), bottom(3)], [bottom(1)], [top(3)], [top(0), bottom(0)]]


def pick(k, values):
    chosen = values[0]
    for at in range(1, len(values)):
        chosen = jnp.where(k == at, values[at], chosen)
    return chosen


def cost(products):
    return pl.CostEstimate(flops=4 * products, bytes_accessed=products // 512, transcendentals=0)


def turned(slot, m):
    return slot ^ ((slot & 1) * m[1])


def a_block(xs, yh, m):
    i = (turned(xs, m) * 2 + yh) ^ m[0]
    return i // 4 * 4 + turned(i % 4, m)


def w_block(ylo, zs, m):
    i = (ylo * 4 + turned(zs, m)) ^ m[0]
    return turned(i // 2, m), i % 2


def sub_of(yh, ylo, m):
    return turned(yh * 2 + ylo, m)


def put(step, groups, outs, store):
    at = 0
    for group, out in zip(groups, outs, strict=True):
        for place in range(len(group)):

            @pl.when(step == at)
            def _():
                store(out.at[place])

            at += 1


def dw_kernel(groups, m, a, g, *outs):
    block = lax.dot_general(a[0], g[...], (((0,), (0,)), ((), ())), preferred_element_type=F32).astype(BF16)
    cols = block.shape[1] // 2

    def store(out):
        out[0] = block[:, :cols]
        out[1] = block[:, cols:]

    put(pl.program_id(0), groups, outs, store)


def weight_terms(scalars, a, g):
    _, t, d = a.shape
    cols = g.shape[1] // 2
    groups = pieces_of(lambda slot: (slot, 0), lambda slot: (slot, 1))
    blocks = sum(groups, [])

    def a_index(k, m):
        return (a_block(pick(k, [b[0] for b in blocks]), pick(k, [b[1] for b in blocks]), m), 0, 0)

    return pl.pallas_call(
        functools.partial(dw_kernel, groups),
        grid_spec=pltpu.PrefetchScalarGridSpec(
            num_scalar_prefetch=1,
            grid=(8,),
            in_specs=[pl.BlockSpec((1, t, d), a_index), pl.BlockSpec(g.shape, lambda k, m: (0, 0))],
            out_specs=[pl.BlockSpec((len(group), 2, d, cols), lambda k, m: (0, 0, 0, 0)) for group in groups],
        ),
        out_shape=[jax.ShapeDtypeStruct((len(group), 2, d, cols), BF16) for group in groups],
        compiler_params=pltpu.CompilerParams(vmem_limit_bytes=32 << 20),
        cost_estimate=cost(8 * t * d * 2 * cols),
        name="weight_terms",
    )(scalars, a, g)


def da_kernel(groups, m, g, w0, w1, *outs):
    rows = jnp.concatenate([w0[0, 0], w1[0, 0]], 1)
    block = lax.dot_general(g[...], rows, (((1,), (1,)), ((), ())), preferred_element_type=F32).astype(BF16)

    def store(out):
        out[...] = block

    put(pl.program_id(0), groups, outs, store)


def input_terms(scalars, g, w):
    t, d, cols = g.shape[0], w.shape[2], w.shape[3]
    groups = pieces_of(lambda slot: (0, slot), lambda slot: (1, slot))
    blocks = sum(groups, [])

    def w_index(ylo, k, m):
        xs, yh = w_block(pick(k, [b[0] for b in blocks]), pick(k, [b[1] for b in blocks]), m)
        return (xs, sub_of(yh, ylo, m), 0, 0)

    return pl.pallas_call(
        functools.partial(da_kernel, groups),
        grid_spec=pltpu.PrefetchScalarGridSpec(
            num_scalar_prefetch=1,
            grid=(8,),
            in_specs=[
                pl.BlockSpec(g.shape, lambda k, m: (0, 0)),
                pl.BlockSpec((1, 1, d, cols), functools.partial(w_index, 0)),
                pl.BlockSpec((1, 1, d, cols), functools.partial(w_index, 1)),
            ],
            out_specs=[pl.BlockSpec((len(group), t, d), lambda k, m: (0, 0, 0)) for group in groups],
        ),
        out_shape=[jax.ShapeDtypeStruct((len(group), t, d), BF16) for group in groups],
        compiler_params=pltpu.CompilerParams(vmem_limit_bytes=32 << 20),
        cost_estimate=cost(8 * t * d * 2 * cols),
        name="input_terms",
    )(scalars, g, w, w)


def fwd_kernel(m, a, w, mine, theirs, rows):
    n, d = a.shape[0], a.shape[2]
    cols = w.shape[-1]

    @pl.when(pl.program_id(0) == 0)
    def _():
        for k in range(n):
            for ylo in range(2):
                rows[k * d : (k + 1) * d, ylo * cols : (ylo + 1) * cols] = w[k // 2, sub_of(k % 2, ylo, m)]

    left = jnp.concatenate([a[a_block(k // 2, k % 2, m)] for k in range(n)], 1)
    block = jnp.dot(left, rows[...], preferred_element_type=F32).astype(BF16)

    @pl.when(pl.program_id(0) < 2)
    def _():
        theirs[...] = block

    @pl.when(pl.program_id(0) >= 2)
    def _():
        mine[...] = block


def forward_terms(scalars, a, w):
    n, t, d = a.shape
    cols = w.shape[3]
    return pl.pallas_call(
        fwd_kernel,
        grid_spec=pltpu.PrefetchScalarGridSpec(
            num_scalar_prefetch=1,
            grid=(4,),
            in_specs=[
                pl.BlockSpec((n, t // 4, d), lambda i, m: (0, (i + 2) % 4, 0)),
                pl.BlockSpec(w.shape, lambda i, m: (0, 0, 0, 0)),
            ],
            out_specs=[
                pl.BlockSpec((t // 4, 2 * cols), lambda i, m: (jnp.maximum(i - 2, 0), 0)),
                pl.BlockSpec((t // 4, 2 * cols), lambda i, m: (jnp.minimum(i, 1), 0)),
            ],
            scratch_shapes=[pltpu.VMEM((n * d, 2 * cols), BF16)],
        ),
        out_shape=[jax.ShapeDtypeStruct((t // 2, 2 * cols), BF16)] * 2,
        compiler_params=pltpu.CompilerParams(vmem_limit_bytes=40 << 20),
        cost_estimate=cost(8 * t * d * 2 * cols),
        name="forward_terms",
    )(scalars, a, w)


def body(activations, qkv_weight, qkv_grad):
    p, q = lax.axis_index("fsdp"), lax.axis_index("node")
    x, y_hi, c, y_lo, z = p // 4, p // 2 % 2, p % 2, q // 4, q % 4
    mask = (x // 2 ^ y_lo) * 4 + (x % 2 ^ z // 2) * 2 + (y_hi ^ z % 2)
    scalars = jnp.stack([mask, 2 * c]).astype(jnp.int32)
    tok, wide = activations.shape
    cols = qkv_grad.shape[1]
    sub = wide // 4

    w_same = lax.dynamic_slice_in_dim(qkv_weight, y_lo * sub, sub, 0)
    w_diff = lax.dynamic_slice_in_dim(qkv_weight, (1 - y_lo) * sub, sub, 0)
    ws_one, ws_two = flip(w_same, x=ONE), flip(w_same, x=TWO)
    w_one, w_two = flip(w_diff, y=ONE), flip(w_diff, y=TWO)
    ws_one, ws_two, w_same = tie(ws_one, ws_two, w_same)
    w_far = flip(w_same, y=2)

    halves = [activations[:, : 2 * sub], activations[:, 2 * sub :]]
    a_mine, a_theirs = jnp.where(c == 0, halves[0], halves[1]), jnp.where(c == 0, halves[1], halves[0])
    a_rows = jnp.concatenate([a_mine, flip(a_theirs, c=1)], 0)
    a_keep = lax.dynamic_slice_in_dim(a_rows, y_lo * sub, sub, 1)
    a_send = lax.dynamic_slice_in_dim(a_rows, (1 - y_lo) * sub, sub, 1)
    w_one, a_send = tie(w_one, a_send)
    a_y = flip(a_send, y=1)
    w_near = jnp.concatenate([w_one, w_far, w_two], 0)
    wn_one, wn_two = flip(w_near, x=ONE), flip(w_near, x=TWO)
    ka_one, ka_two = flip(a_keep, z=ONE), flip(a_keep, z=TWO)
    a_y, grad = tie(a_y, qkv_grad)
    g_y = flip(grad, y=1)
    ya_one, ya_two = flip(a_y, z=ONE), flip(a_y, z=TWO)
    far_one, far_two = flip(ka_two[:tok], z=ONE), flip(ka_one[tok:], z=TWO)
    ka_far = jnp.concatenate([far_one, far_two], 0)
    far_one, far_two = flip(ya_two[:tok], z=ONE), flip(ya_one[tok:], z=TWO)
    ya_far = jnp.concatenate([far_one, far_two], 0)
    a = jnp.stack([a_keep, ka_one, ka_far, ka_two, a_y, ya_one, ya_far, ya_two])

    w_own, w_1, w_2 = (jnp.concatenate(v, 0) for v in ((w_same, w_near), (ws_one, wn_one), (ws_two, wn_two)))
    far_one, far_two = flip(w_2[: 2 * sub], x=ONE), flip(w_1[2 * sub :], x=TWO)
    g_rows = jnp.concatenate([grad, g_y], 1)
    g = jnp.concatenate([g_rows, flip(g_rows, c=1)], 0)

    dw_first, *dw = weight_terms(scalars, a, g)
    dw_first, far_one, far_two = tie(dw_first, far_one, far_two)
    w = jnp.stack([w_own, w_1, jnp.concatenate([far_one, far_two], 0), w_2]).reshape(4, 4, sub, cols)
    da_first, *da = input_terms(scalars, g, w)
    da_first, scalars = tie(da_first, scalars)
    da_keep, da_send = scatter4(da_first, *da, "z")
    dw_0, dw_1 = scatter4(dw_first, *dw, "x")

    mine, theirs = forward_terms(scalars, a, w)
    fwd = add(mine, flip(theirs, c=1))
    fwd_y = flip(fwd[:, cols:].astype(BF16), y=1)
    fwd_y, da_send = tie(fwd_y, da_send)
    projected = add(fwd[:, :cols], fwd_y).astype(BF16)

    da_y = flip(da_send.astype(BF16), y=1)
    da_keep = da_keep.astype(BF16)
    r0, r1 = jnp.where(y_lo == 0, da_keep, da_y), jnp.where(y_lo == 0, da_y, da_keep)
    both = jnp.concatenate([r0, r1], 1)
    mine, theirs = both[:tok], flip(both[tok:], c=1)
    input_grad = jnp.concatenate([jnp.where(c == 0, mine, theirs), jnp.where(c == 0, theirs, mine)], 1)

    send1, send3 = dw_0[1].astype(BF16), dw_1[1].astype(BF16)
    got_one = flip(jnp.where(c == 0, send1, send3), y=ONE)
    got_two = flip(jnp.where(c == 0, send3, send1), y=TWO)
    got_far = flip(dw_1[0].astype(BF16), y=2)
    same, diff = add(dw_0[0], got_far), add(got_one, got_two)
    weight_grad = jnp.where(y_lo == 0, jnp.concatenate([same, diff], 0), jnp.concatenate([diff, same], 0))

    return projected, input_grad, weight_grad


def solution(mesh):
    spec = P("fsdp", "node")
    return jax.shard_map(body, mesh=mesh, in_specs=(spec,) * 3, out_specs=(spec,) * 3, check_vma=False)
```

```python
import functools

import jax
import jax.numpy as jnp
from jax import lax
from jax.experimental import pallas as pl
from jax.experimental.pallas import tpu as pltpu
from jax.sharding import PartitionSpec as P

AXES = ("fsdp", "node")
BF16, F32 = jnp.bfloat16, jnp.float32
FAR = 2


def flip(value, x=0, y=0, z=0, c=0):
    pairs = []
    for i in range(128):
        p, q = divmod(i, 8)
        place = p // 4, (p // 2 % 2) * 2 + q // 4, q % 4, p % 2
        bits = [b if isinstance(b, int) else b[place[3]] for b in (x, y, z, c)]
        px, py, pz, pc = (a ^ b for a, b in zip(place, bits, strict=True))
        pairs.append((i, ((px * 2 + py // 2) * 2 + pc) * 8 + py % 2 * 4 + pz))
    return lax.ppermute(value, AXES, pairs)


ONE, TWO = (1, 3), (3, 1)


def tie(*values):
    return lax.optimization_barrier(values)


def add(*terms):
    total = terms[0].astype(F32)
    for term in terms[1:]:
        total = total + term.astype(F32)
    return total


def gather4(value, axis):
    one, two = flip(value, **{axis: ONE}), flip(value, **{axis: TWO})
    half = value.shape[0] // 2
    far = [flip(two[:half], **{axis: ONE}), flip(one[half:], **{axis: TWO})]
    return [value, one, jnp.concatenate(far, 0), two]


def scatter_start(far_one, far_two, axis):
    return flip(far_one, **{axis: ONE}), flip(far_two, **{axis: TWO})


def scatter_add(got_one, got_two, one, two):
    return add(one[0], got_two[0]).astype(BF16), add(two[0], got_one[0]).astype(BF16)


def scatter_end(got_one, got_two, send_one, send_two, own, axis):
    got_bottom1, got_top2 = flip(send_one, **{axis: ONE}), flip(send_two, **{axis: TWO})
    return add(own[0], got_one[1], got_top2), add(own[1], got_two[1], got_bottom1)


def pieces_of(top, bottom):
    return [[top(2), top(1)], [bottom(2), bottom(3)], [bottom(1)], [top(3)], [top(0), bottom(0)]]


def pick(k, values):
    chosen = values[0]
    for at in range(1, len(values)):
        chosen = jnp.where(k == at, values[at], chosen)
    return chosen


def cost(products, factor):
    return pl.CostEstimate(flops=int(factor * products), bytes_accessed=int(factor * products) // 2048, transcendentals=0)


def turned(slot, m):
    return slot ^ ((slot & 1) * m[1])


def a_block(xs, yh, m):
    i = (turned(xs, m) * 2 + yh) ^ m[0]
    return i // 4 * 4 + turned(i % 4, m)


def w_block(ylo, zs, m):
    i = (ylo * 4 + turned(zs, m)) ^ m[0]
    return turned(i // 2, m), i % 2


def sub_of(yh, ylo, m):
    return turned(yh * 2 + ylo, m)


def put(step, groups, outs, store):
    at = 0
    for group, out in zip(groups, outs, strict=True):
        for place in range(len(group)):

            @pl.when(step == at)
            def _():
                store(out.at[place])

            at += 1


def dw_kernel(groups, m, a, g, *outs):
    block = lax.dot_general(a[0], g[...], (((0,), (0,)), ((), ())), preferred_element_type=F32).astype(BF16)
    cols = block.shape[1] // 2

    def store(out):
        out[0] = block[:, :cols]
        out[1] = block[:, cols:]

    put(pl.program_id(0), groups, outs, store)


def weight_terms(scalars, a, g):
    _, t, d = a.shape
    cols = g.shape[1] // 2
    groups = pieces_of(lambda slot: (slot, 0), lambda slot: (slot, 1))
    blocks = sum(groups, [])

    def a_index(k, m):
        return (a_block(pick(k, [b[0] for b in blocks]), pick(k, [b[1] for b in blocks]), m), 0, 0)

    return pl.pallas_call(
        functools.partial(dw_kernel, groups),
        grid_spec=pltpu.PrefetchScalarGridSpec(
            num_scalar_prefetch=1,
            grid=(8,),
            in_specs=[pl.BlockSpec((1, t, d), a_index), pl.BlockSpec(g.shape, lambda k, m: (0, 0))],
            out_specs=[pl.BlockSpec((len(group), 2, d, cols), lambda k, m: (0, 0, 0, 0)) for group in groups],
        ),
        out_shape=[jax.ShapeDtypeStruct((len(group), 2, d, cols), BF16) for group in groups],
        compiler_params=pltpu.CompilerParams(vmem_limit_bytes=32 << 20),
        cost_estimate=cost(8 * t * d * 2 * cols, 2),
        name="weight_terms",
    )(scalars, a, g)


def da_kernel(groups, m, g, w0, w1, *outs):
    rows = jnp.concatenate([w0[0, 0], w1[0, 0]], 1)
    block = lax.dot_general(g[...], rows, (((1,), (1,)), ((), ())), preferred_element_type=F32).astype(BF16)

    def store(out):
        out[...] = block

    put(pl.program_id(0), groups, outs, store)


def input_terms(scalars, g, w):
    t, d, cols = g.shape[0], w.shape[2], w.shape[3]
    groups = pieces_of(lambda slot: (0, slot), lambda slot: (1, slot))
    blocks = sum(groups, [])

    def w_index(ylo, k, m):
        xs, yh = w_block(pick(k, [b[0] for b in blocks]), pick(k, [b[1] for b in blocks]), m)
        return (xs, sub_of(yh, ylo, m), 0, 0)

    return pl.pallas_call(
        functools.partial(da_kernel, groups),
        grid_spec=pltpu.PrefetchScalarGridSpec(
            num_scalar_prefetch=1,
            grid=(8,),
            in_specs=[
                pl.BlockSpec(g.shape, lambda k, m: (0, 0)),
                pl.BlockSpec((1, 1, d, cols), functools.partial(w_index, 0)),
                pl.BlockSpec((1, 1, d, cols), functools.partial(w_index, 1)),
            ],
            out_specs=[pl.BlockSpec((len(group), t, d), lambda k, m: (0, 0, 0)) for group in groups],
        ),
        out_shape=[jax.ShapeDtypeStruct((len(group), t, d), BF16) for group in groups],
        compiler_params=pltpu.CompilerParams(vmem_limit_bytes=32 << 20),
        cost_estimate=cost(8 * t * d * 2 * cols, 8),
        name="input_terms",
    )(scalars, g, w, w)


def fwd_kernel(m, a, w, mine, theirs, rows):
    n, d = a.shape[0], a.shape[2]
    cols = w.shape[-1]

    @pl.when(pl.program_id(0) == 0)
    def _():
        for k in range(n):
            for ylo in range(2):
                rows[k * d : (k + 1) * d, ylo * cols : (ylo + 1) * cols] = w[k // 2, sub_of(k % 2, ylo, m)]

    left = jnp.concatenate([a[a_block(k // 2, k % 2, m)] for k in range(n)], 1)
    block = jnp.dot(left, rows[...], preferred_element_type=F32).astype(BF16)

    @pl.when(pl.program_id(0) < 2)
    def _():
        theirs[...] = block

    @pl.when(pl.program_id(0) >= 2)
    def _():
        mine[...] = block


def forward_terms(scalars, a, w):
    n, t, d = a.shape
    cols = w.shape[3]
    return pl.pallas_call(
        fwd_kernel,
        grid_spec=pltpu.PrefetchScalarGridSpec(
            num_scalar_prefetch=1,
            grid=(4,),
            in_specs=[
                pl.BlockSpec((n, t // 4, d), lambda i, m: (0, (i + 2) % 4, 0)),
                pl.BlockSpec(w.shape, lambda i, m: (0, 0, 0, 0)),
            ],
            out_specs=[
                pl.BlockSpec((t // 4, 2 * cols), lambda i, m: (jnp.maximum(i - 2, 0), 0)),
                pl.BlockSpec((t // 4, 2 * cols), lambda i, m: (jnp.minimum(i, 1), 0)),
            ],
            scratch_shapes=[pltpu.VMEM((n * d, 2 * cols), BF16)],
        ),
        out_shape=[jax.ShapeDtypeStruct((t // 2, 2 * cols), BF16)] * 2,
        compiler_params=pltpu.CompilerParams(vmem_limit_bytes=40 << 20),
        cost_estimate=cost(8 * t * d * 2 * cols, 2),
        name="forward_terms",
    )(scalars, a, w)


def body(activations, qkv_weight, qkv_grad):
    p, q = lax.axis_index("fsdp"), lax.axis_index("node")
    x, y_hi, c, y_lo, z = p // 4, p // 2 % 2, p % 2, q // 4, q % 4
    mask = (x // 2 ^ y_lo) * 4 + (x % 2 ^ z // 2) * 2 + (y_hi ^ z % 2)
    scalars = jnp.stack([mask, 2 * c]).astype(jnp.int32)
    tok, wide = activations.shape
    cols = qkv_grad.shape[1]
    sub = wide // 4

    w_same = lax.dynamic_slice_in_dim(qkv_weight, y_lo * sub, sub, 0)
    w_diff = lax.dynamic_slice_in_dim(qkv_weight, (1 - y_lo) * sub, sub, 0)
    ws_one, ws_two = flip(w_same, x=ONE), flip(w_same, x=TWO)
    w_one, w_two = flip(w_diff, y=ONE), flip(w_diff, y=TWO)
    w_far = flip(w_same, y=2)

    halves = [activations[:, : 2 * sub], activations[:, 2 * sub :]]
    a_mine, a_theirs = jnp.where(c == 0, halves[0], halves[1]), jnp.where(c == 0, halves[1], halves[0])
    a_rows = jnp.concatenate([a_mine, flip(a_theirs, c=1)], 0)
    a_keep = lax.dynamic_slice_in_dim(a_rows, y_lo * sub, sub, 1)
    a_send = lax.dynamic_slice_in_dim(a_rows, (1 - y_lo) * sub, sub, 1)
    ws_one, ws_two, a_keep = tie(ws_one, ws_two, a_keep)
    w_far, a_send = tie(w_far, a_send)
    a_y = flip(a_send, y=1)
    w_near = jnp.concatenate([w_one, w_far, w_two], 0)
    wn_one, wn_two = flip(w_near, x=ONE), flip(w_near, x=TWO)
    ka_one, ka_two = flip(a_keep, z=ONE), flip(a_keep, z=TWO)
    grad = qkv_grad
    a_y, grad = tie(a_y, grad)
    g_y = flip(grad, y=1)
    ya_one, ya_two = flip(a_y, z=ONE), flip(a_y, z=TWO)
    far_one, far_two = flip(ka_two[:tok], z=ONE), flip(ka_one[tok:], z=TWO)
    ka_far = jnp.concatenate([far_one, far_two], 0)
    far_one, far_two = flip(ya_two[:tok], z=ONE), flip(ya_one[tok:], z=TWO)
    ya_far = jnp.concatenate([far_one, far_two], 0)
    a = jnp.stack([a_keep, ka_one, ka_far, ka_two, a_y, ya_one, ya_far, ya_two])

    w_own, w_1, w_2 = (jnp.concatenate(v, 0) for v in ((w_same, w_near), (ws_one, wn_one), (ws_two, wn_two)))
    far_one, far_two = flip(w_2[: 2 * sub], x=ONE), flip(w_1[2 * sub :], x=TWO)
    g_rows = jnp.concatenate([grad, g_y], 1)
    g = jnp.concatenate([g_rows, flip(g_rows, c=1)], 0)

    dw_first, *dw = weight_terms(scalars, a, g)
    dw_first, far_one, far_two = tie(dw_first, far_one, far_two)
    w = jnp.stack([w_own, w_1, jnp.concatenate([far_one, far_two], 0), w_2]).reshape(4, 4, sub, cols)
    da_first, *da = input_terms(scalars, g, w)
    da_first, scalars = tie(da_first, scalars)
    dw_got = scatter_start(dw_first, dw[0], "x")
    da_got = scatter_start(da_first, da[0], "z")
    dw_sum = scatter_add(*dw_got, dw[1], dw[2])
    da_sum = scatter_add(*da_got, da[1], da[2])
    dw_0, dw_1 = scatter_end(*dw_got, *dw_sum, dw[3], "x")
    da_keep, da_send = scatter_end(*da_got, *da_sum, da[3], "z")
    da_keep, da_send = da_keep.astype(BF16), da_send.astype(BF16)
    dw_send = [dw_0[1].astype(BF16), dw_1[1].astype(BF16), dw_1[0].astype(BF16)]

    mine, theirs = forward_terms(scalars, a, w)
    got = flip(theirs, c=1)
    fwd = add(mine, got)
    fwd_y = flip(fwd[:, cols:].astype(BF16), y=1)
    fwd_y, da_send = tie(fwd_y, da_send)
    projected = add(fwd[:, :cols], fwd_y).astype(BF16)

    def by_r(keep, other):
        return jnp.concatenate([jnp.where(y_lo == 0, keep, other), jnp.where(y_lo == 0, other, keep)], 1)

    da_y = flip(da_send, y=1)
    both = by_r(da_keep, da_y)
    mine, theirs = both[:tok], flip(both[tok:], c=1)
    input_grad = jnp.concatenate([jnp.where(c == 0, mine, theirs), jnp.where(c == 0, theirs, mine)], 1)

    send1, send3, send2 = dw_send
    got_one = flip(jnp.where(c == 0, send1, send3), y=ONE)
    got_two = flip(jnp.where(c == 0, send3, send1), y=TWO)
    got_far = flip(send2, y=2)
    same, diff = add(dw_0[0], got_far), add(got_one, got_two)
    weight_grad = jnp.where(y_lo == 0, jnp.concatenate([same, diff], 0), jnp.concatenate([diff, same], 0))
    return projected, input_grad, weight_grad


def solution(mesh):
    spec = P("fsdp", "node")
    return jax.shard_map(body, mesh=mesh, in_specs=(spec,) * 3, out_specs=(spec,) * 3, check_vma=False)
```

```python
import functools

import jax
import jax.numpy as jnp
from jax import lax
from jax.experimental import pallas as pl
from jax.experimental.pallas import tpu as pltpu
from jax.sharding import PartitionSpec as P

AXES = ("fsdp", "node")
BF16, F32 = jnp.bfloat16, jnp.float32
FAR = 2


def flip(value, x=0, y=0, z=0, c=0):
    pairs = []
    for i in range(128):
        p, q = divmod(i, 8)
        place = p // 4, (p // 2 % 2) * 2 + q // 4, q % 4, p % 2
        bits = [b if isinstance(b, int) else b[place[3]] for b in (x, y, z, c)]
        px, py, pz, pc = (a ^ b for a, b in zip(place, bits, strict=True))
        pairs.append((i, ((px * 2 + py // 2) * 2 + pc) * 8 + py % 2 * 4 + pz))
    return lax.ppermute(value, AXES, pairs)


ONE, TWO = (1, 3), (3, 1)


def tie(*values):
    return lax.optimization_barrier(values)


def add(*terms):
    total = terms[0].astype(F32)
    for term in terms[1:]:
        total = total + term.astype(F32)
    return total


def gather4(value, axis):
    one, two = flip(value, **{axis: ONE}), flip(value, **{axis: TWO})
    half = value.shape[0] // 2
    far = [flip(two[:half], **{axis: ONE}), flip(one[half:], **{axis: TWO})]
    return [value, one, jnp.concatenate(far, 0), two]


def scatter_start(far_one, far_two, axis):
    return flip(far_one, **{axis: ONE}), flip(far_two, **{axis: TWO})


def scatter_add(got_one, got_two, one, two):
    return add(one[0], got_two[0]).astype(BF16), add(two[0], got_one[0]).astype(BF16)


def scatter_end(got_one, got_two, send_one, send_two, own, axis):
    got_bottom1, got_top2 = flip(send_one, **{axis: ONE}), flip(send_two, **{axis: TWO})
    return add(own[0], got_one[1], got_top2), add(own[1], got_two[1], got_bottom1)


def pieces_of(top, bottom):
    return [[top(2), top(1)], [bottom(2), bottom(3)], [bottom(1)], [top(3)], [top(0), bottom(0)]]


def pick(k, values):
    chosen = values[0]
    for at in range(1, len(values)):
        chosen = jnp.where(k == at, values[at], chosen)
    return chosen


def cost(products, factor):
    return pl.CostEstimate(flops=int(factor * products), bytes_accessed=int(factor * products) // 2048, transcendentals=0)


def turned(slot, m):
    return slot ^ ((slot & 1) * m[1])


def a_block(xs, yh, m):
    i = (turned(xs, m) * 2 + yh) ^ m[0]
    return i // 4 * 4 + turned(i % 4, m)


def w_block(ylo, zs, m):
    i = (ylo * 4 + turned(zs, m)) ^ m[0]
    return turned(i // 2, m), i % 2


def sub_of(yh, ylo, m):
    return turned(yh * 2 + ylo, m)


def put(step, groups, outs, store):
    at = 0
    for group, out in zip(groups, outs, strict=True):
        for place in range(len(group)):

            @pl.when(step == at)
            def _():
                store(out.at[0])

            at += 1


def out_specs(groups, shape):
    specs, first = [], 0
    for group in groups:

        def index(k, m, first=first, last=len(group) - 1):
            return (jnp.clip(k - first, 0, last), *(0 for _ in shape))

        specs.append(pl.BlockSpec((1, *shape), index))
        first += len(group)
    return specs


def dw_kernel(groups, m, a, g, *outs):
    block = lax.dot_general(a[0], g[...], (((0,), (0,)), ((), ())), preferred_element_type=F32).astype(BF16)
    cols = block.shape[1] // 2

    def store(out):
        out[0] = block[:, :cols]
        out[1] = block[:, cols:]

    put(pl.program_id(0), groups, outs, store)


def weight_terms(scalars, a, g):
    _, t, d = a.shape
    cols = g.shape[1] // 2
    groups = pieces_of(lambda slot: (slot, 0), lambda slot: (slot, 1))
    blocks = sum(groups, [])

    def a_index(k, m):
        return (a_block(pick(k, [b[0] for b in blocks]), pick(k, [b[1] for b in blocks]), m), 0, 0)

    return pl.pallas_call(
        functools.partial(dw_kernel, groups),
        grid_spec=pltpu.PrefetchScalarGridSpec(
            num_scalar_prefetch=1,
            grid=(8,),
            in_specs=[pl.BlockSpec((1, t, d), a_index), pl.BlockSpec(g.shape, lambda k, m: (0, 0))],
            out_specs=out_specs(groups, (2, d, cols)),
        ),
        out_shape=[jax.ShapeDtypeStruct((len(group), 2, d, cols), BF16) for group in groups],
        compiler_params=pltpu.CompilerParams(vmem_limit_bytes=32 << 20),
        cost_estimate=cost(8 * t * d * 2 * cols, 2),
        name="weight_terms",
    )(scalars, a, g)


def da_kernel(groups, m, g, w0, w1, *outs):
    rows = jnp.concatenate([w0[0, 0], w1[0, 0]], 1)
    block = lax.dot_general(g[...], rows, (((1,), (1,)), ((), ())), preferred_element_type=F32).astype(BF16)

    def store(out):
        out[...] = block

    put(pl.program_id(0), groups, outs, store)


def input_terms(scalars, g, w):
    t, d, cols = g.shape[0], w.shape[2], w.shape[3]
    groups = pieces_of(lambda slot: (0, slot), lambda slot: (1, slot))
    blocks = sum(groups, [])

    def w_index(ylo, k, m):
        xs, yh = w_block(pick(k, [b[0] for b in blocks]), pick(k, [b[1] for b in blocks]), m)
        return (xs, sub_of(yh, ylo, m), 0, 0)

    return pl.pallas_call(
        functools.partial(da_kernel, groups),
        grid_spec=pltpu.PrefetchScalarGridSpec(
            num_scalar_prefetch=1,
            grid=(8,),
            in_specs=[
                pl.BlockSpec(g.shape, lambda k, m: (0, 0)),
                pl.BlockSpec((1, 1, d, cols), functools.partial(w_index, 0)),
                pl.BlockSpec((1, 1, d, cols), functools.partial(w_index, 1)),
            ],
            out_specs=out_specs(groups, (t, d)),
        ),
        out_shape=[jax.ShapeDtypeStruct((len(group), t, d), BF16) for group in groups],
        compiler_params=pltpu.CompilerParams(vmem_limit_bytes=32 << 20),
        cost_estimate=cost(8 * t * d * 2 * cols, 8),
        name="input_terms",
    )(scalars, g, w, w)


def fwd_kernel(m, a, w, mine, theirs, rows):
    n, d = a.shape[0], a.shape[2]
    cols = w.shape[-1]

    @pl.when(pl.program_id(0) == 0)
    def _():
        for k in range(n):
            for ylo in range(2):
                rows[k * d : (k + 1) * d, ylo * cols : (ylo + 1) * cols] = w[k // 2, sub_of(k % 2, ylo, m)]

    left = jnp.concatenate([a[a_block(k // 2, k % 2, m)] for k in range(n)], 1)
    block = jnp.dot(left, rows[...], preferred_element_type=F32).astype(BF16)

    @pl.when(pl.program_id(0) < 2)
    def _():
        theirs[...] = block

    @pl.when(pl.program_id(0) >= 2)
    def _():
        mine[...] = block


def forward_terms(scalars, a, w):
    n, t, d = a.shape
    cols = w.shape[3]
    return pl.pallas_call(
        fwd_kernel,
        grid_spec=pltpu.PrefetchScalarGridSpec(
            num_scalar_prefetch=1,
            grid=(4,),
            in_specs=[
                pl.BlockSpec((n, t // 4, d), lambda i, m: (0, (i + 2) % 4, 0)),
                pl.BlockSpec(w.shape, lambda i, m: (0, 0, 0, 0)),
            ],
            out_specs=[
                pl.BlockSpec((t // 4, 2 * cols), lambda i, m: (jnp.maximum(i - 2, 0), 0)),
                pl.BlockSpec((t // 4, 2 * cols), lambda i, m: (jnp.minimum(i, 1), 0)),
            ],
            scratch_shapes=[pltpu.VMEM((n * d, 2 * cols), BF16)],
        ),
        out_shape=[jax.ShapeDtypeStruct((t // 2, 2 * cols), BF16)] * 2,
        compiler_params=pltpu.CompilerParams(vmem_limit_bytes=40 << 20),
        cost_estimate=cost(8 * t * d * 2 * cols, 2),
        name="forward_terms",
    )(scalars, a, w)


def body(activations, qkv_weight, qkv_grad):
    p, q = lax.axis_index("fsdp"), lax.axis_index("node")
    x, y_hi, c, y_lo, z = p // 4, p // 2 % 2, p % 2, q // 4, q % 4
    mask = (x // 2 ^ y_lo) * 4 + (x % 2 ^ z // 2) * 2 + (y_hi ^ z % 2)
    scalars = jnp.stack([mask, 2 * c]).astype(jnp.int32)
    tok, wide = activations.shape
    cols = qkv_grad.shape[1]
    sub = wide // 4

    w_same = lax.dynamic_slice_in_dim(qkv_weight, y_lo * sub, sub, 0)
    w_diff = lax.dynamic_slice_in_dim(qkv_weight, (1 - y_lo) * sub, sub, 0)
    ws_one, ws_two = flip(w_same, x=ONE), flip(w_same, x=TWO)
    w_one, w_two = flip(w_diff, y=ONE), flip(w_diff, y=TWO)
    w_far = flip(w_same, y=2)

    halves = [activations[:, : 2 * sub], activations[:, 2 * sub :]]
    a_mine, a_theirs = jnp.where(c == 0, halves[0], halves[1]), jnp.where(c == 0, halves[1], halves[0])
    a_rows = jnp.concatenate([a_mine, flip(a_theirs, c=1)], 0)
    a_keep = lax.dynamic_slice_in_dim(a_rows, y_lo * sub, sub, 1)
    a_send = lax.dynamic_slice_in_dim(a_rows, (1 - y_lo) * sub, sub, 1)
    ws_one, ws_two, a_keep = tie(ws_one, ws_two, a_keep)
    w_far, a_send = tie(w_far, a_send)
    a_y = flip(a_send, y=1)
    w_near = jnp.concatenate([w_one, w_far, w_two], 0)
    wn_one, wn_two = flip(w_near, x=ONE), flip(w_near, x=TWO)
    ka_one, ka_two = flip(a_keep, z=ONE), flip(a_keep, z=TWO)
    grad = qkv_grad
    a_y, grad = tie(a_y, grad)
    g_y = flip(grad, y=1)
    ya_one, ya_two = flip(a_y, z=ONE), flip(a_y, z=TWO)
    far_one, far_two = flip(ka_two[:tok], z=ONE), flip(ka_one[tok:], z=TWO)
    ka_far = jnp.concatenate([far_one, far_two], 0)
    far_one, far_two = flip(ya_two[:tok], z=ONE), flip(ya_one[tok:], z=TWO)
    ya_far = jnp.concatenate([far_one, far_two], 0)
    a = jnp.stack([a_keep, ka_one, ka_far, ka_two, a_y, ya_one, ya_far, ya_two])

    w_own, w_1, w_2 = (jnp.concatenate(v, 0) for v in ((w_same, w_near), (ws_one, wn_one), (ws_two, wn_two)))
    far_one, far_two = flip(w_2[: 2 * sub], x=ONE), flip(w_1[2 * sub :], x=TWO)
    g_rows = jnp.concatenate([grad, g_y], 1)
    g = jnp.concatenate([g_rows, flip(g_rows, c=1)], 0)

    dw_first, *dw = weight_terms(scalars, a, g)
    dw_first, far_one, far_two = tie(dw_first, far_one, far_two)
    w = jnp.stack([w_own, w_1, jnp.concatenate([far_one, far_two], 0), w_2]).reshape(4, 4, sub, cols)
    da_first, *da = input_terms(scalars, g, w)
    da_first, scalars = tie(da_first, scalars)
    dw_got = scatter_start(dw_first, dw[0], "x")
    da_got = scatter_start(da_first, da[0], "z")
    dw_sum = scatter_add(*dw_got, dw[1], dw[2])
    da_sum = scatter_add(*da_got, da[1], da[2])
    dw_0, dw_1 = scatter_end(*dw_got, *dw_sum, dw[3], "x")
    da_keep, da_send = scatter_end(*da_got, *da_sum, da[3], "z")
    da_keep, da_send = da_keep.astype(BF16), da_send.astype(BF16)
    dw_send = [dw_0[1].astype(BF16), dw_1[1].astype(BF16), dw_1[0].astype(BF16)]

    mine, theirs = forward_terms(scalars, a, w)
    got = flip(theirs, c=1)
    fwd = add(mine, got)
    fwd_y = flip(fwd[:, cols:].astype(BF16), y=1)
    fwd_y, da_send = tie(fwd_y, da_send)
    projected = add(fwd[:, :cols], fwd_y).astype(BF16)

    def by_r(keep, other):
        return jnp.concatenate([jnp.where(y_lo == 0, keep, other), jnp.where(y_lo == 0, other, keep)], 1)

    da_y = flip(da_send, y=1)
    both = by_r(da_keep, da_y)
    mine, theirs = both[:tok], flip(both[tok:], c=1)
    input_grad = jnp.concatenate([jnp.where(c == 0, mine, theirs), jnp.where(c == 0, theirs, mine)], 1)

    send1, send3, send2 = dw_send
    got_one = flip(jnp.where(c == 0, send1, send3), y=ONE)
    got_two = flip(jnp.where(c == 0, send3, send1), y=TWO)
    got_far = flip(send2, y=2)
    input_grad, got_one, got_two, got_far = tie(input_grad, got_one, got_two, got_far)
    same, diff = add(dw_0[0], got_far), add(got_one, got_two)
    weight_grad = jnp.where(y_lo == 0, jnp.concatenate([same, diff], 0), jnp.concatenate([diff, same], 0))
    return projected, input_grad, weight_grad


def solution(mesh):
    spec = P("fsdp", "node")
    return jax.shard_map(body, mesh=mesh, in_specs=(spec,) * 3, out_specs=(spec,) * 3, check_vma=False)
```
